32 devices in a mesh: group: 4 (over z), shard: 8 (over y, x, core).
Axes of the slice: x: 2, y: 2, z: 4, core: 2. Of those that a mesh axis runs over, the one named last changes fastest.
Arguments:
- hot_row: int32 [256, 39], P(('group', 'shard')), may hold values from 0 to 2047
- cold_row: int32 [256, 39], P(('group', 'shard')), may hold values from 0 to 4095
- cold_owner: int32 [256, 39], P(('group', 'shard')), may hold values from 0 to 7, as said below
- is_cold: int32 [256, 39], P(('group', 'shard')), may hold values from 0 to 1
- grad_logit: float32 [256], P(('group', 'shard')), may hold values from -12 to 12
- hot_table: bfloat16 [2048, 128], replicated, may hold values from -6 to 6
- cold_table: bfloat16 [32768, 128], P('shard'), may hold values from -6 to 6
- first_weight: bfloat16 [100, 1521], replicated, may hold values from -0.15625 to 0.15625
- second_weight: bfloat16 [100, 3900], replicated, may hold values from -0.09375 to 0.09375
- third_weight: bfloat16 [100, 3900], replicated, may hold values from -0.09375 to 0.09375
- out_weight: float32 [3, 100], replicated, may hold values from -0.375 to 0.375
Outputs:
- hot_grad: bfloat16 [2048, 128], replicated
- cold_grad: bfloat16 [32768, 128], P('shard')
- logits: float32 [256], P(('group', 'shard'))
The draws below stay inside these ranges and needn't reach their ends.
Inputs may be any that keep to these rules, and one draw needn't show every extreme that they name: `cold_owner`: among the 312 lookups of one device, at most 39 with is_cold 1 name the same owner; for each index of group, one owner receives exactly 39 such lookups from every device of that group index.
All inputs are finite; a program needn't handle non-finite values.
Results may differ from the reference program's by a relative error of at most 0.014.
Values may be sent and summed in bfloat16 or wider, within the bound.
A program may use at most 64 MiB of HBM per device.

```python
import jax
import jax.numpy as jnp
from jax import lax

E = 128
F = 39
H = 100
B_DEV = 8
HOT_ROWS = 2048
CR_DEV = 4096
SAMPLES = 256
COLD_ROWS = 32768
CAP = 39
N_SHARD = 8


def plan_lookups(key):
    blocks = SAMPLES // B_DEV
    lookups = B_DEV * F
    groups = blocks // N_SHARD
    heavy = jax.random.randint(jax.random.fold_in(key, 11), (groups,), 0, N_SHARD)
    counts = jax.random.randint(jax.random.fold_in(key, 12), (blocks, N_SHARD), 0, CAP + 1)
    block_group = jnp.arange(blocks, dtype=jnp.int32) // N_SHARD
    forced = heavy[block_group][:, None] == jnp.arange(N_SHARD, dtype=jnp.int32)[None, :]
    counts = jnp.where(forced, CAP, counts)
    ends = jnp.cumsum(counts, axis=1)
    totals = ends[:, -1:]
    position = jnp.arange(lookups, dtype=jnp.int32)
    sorted_owner = jnp.sum((ends[:, None, :] <= position[None, :, None]).astype(jnp.int32), axis=2)
    sorted_cold = (position[None, :] < totals).astype(jnp.int32)
    filler = jax.random.randint(jax.random.fold_in(key, 13), (blocks, lookups), 0, N_SHARD)
    sorted_owner = jnp.where(sorted_cold == 1, sorted_owner, filler)
    block_keys = jax.random.split(jax.random.fold_in(key, 14), blocks)
    orders = jax.vmap(lambda block_key: jax.random.permutation(block_key, lookups))(block_keys)
    owner = jnp.take_along_axis(sorted_owner, orders, axis=1)
    coldness = jnp.take_along_axis(sorted_cold, orders, axis=1)
    return (owner.reshape(SAMPLES, F).astype(jnp.int32), coldness.reshape(SAMPLES, F).astype(jnp.int32))


def draw_cold_owner(key, part):
    return plan_lookups(key)[0]


def draw_is_cold(key, part):
    return plan_lookups(key)[1]


def draw_hot_row(key, part):
    blocks = SAMPLES // B_DEV
    upper = jax.random.randint(jax.random.fold_in(key, 21), (SAMPLES, F), 1, HOT_ROWS + 1)
    ranked = jax.random.randint(jax.random.fold_in(key, 22), (SAMPLES, F), 0, upper)
    order = jax.random.permutation(jax.random.fold_in(key, 23), HOT_ROWS).astype(jnp.int32)
    common = order[ranked]
    block_index = jnp.arange(SAMPLES, dtype=jnp.int32) // B_DEV
    start = block_index * HOT_ROWS // blocks
    reach = max(1, HOT_ROWS // blocks)
    offset = jax.random.randint(jax.random.fold_in(key, 24), (SAMPLES, F), 0, reach)
    local = (start[:, None] + offset) % HOT_ROWS
    choose = jax.random.randint(jax.random.fold_in(key, 25), (SAMPLES, F), 0, 2)
    return jnp.where(choose == 1, local, common).astype(jnp.int32)


def touch_ends(array, rng, low, largest):
    longest = array.shape.index(max(array.shape))
    spots = []
    for shift in (0, 1):
        where = [jax.random.randint(jax.random.fold_in(rng, axis), (), 0, length) for axis, length in enumerate(array.shape)]
        where[longest] = (where[longest] + shift) % array.shape[longest]
        spots.append(tuple(where))
    return array.at[spots[0]].set(low).at[spots[1]].set(largest)


def level_of(stream_key, shape, cuts, smallest, top_value):
    def one(dim, blocks):
        draws = jax.random.uniform(jax.random.fold_in(jax.random.fold_in(stream_key, 6), dim), (blocks,), jnp.float32, smallest / len(cuts), top_value / len(cuts))
        return jnp.repeat(jnp.exp(draws), shape[dim] // blocks).reshape((-1,) + (1,) * (len(shape) - dim - 1))

    level = one(*cuts[0])
    for cut in cuts[1:]:
        level = level * one(*cut)
    return level


def centred(rng, extent, width, most, shards=(), held_as=jnp.bfloat16):
    drawn = jax.random.normal(rng, extent, jnp.float32) * width
    if len(shards) > 0:
        drawn = level_of(rng, extent, shards, -0.22, 0.18) * drawn
    return jnp.clip(drawn, min=-most, max=most).astype(held_as)


def setup_inputs(seed: int = 0) -> dict:
    keys = jax.random.split(jax.random.key(seed), 12)
    hot_row = draw_hot_row(jax.random.fold_in(keys[11], 71), 0)
    cold_row = touch_ends(jax.random.randint(keys[1], (SAMPLES, F), 0, CR_DEV), jax.random.fold_in(keys[1], 1), 0, CR_DEV - 1).astype(jnp.int32)
    cold_owner = draw_cold_owner(jax.random.fold_in(keys[11], 71), 0)
    is_cold = draw_is_cold(jax.random.fold_in(keys[11], 71), 0)
    grad_logit = centred(keys[4], (SAMPLES,), 2.0, 12.0, ((0, 32),), jnp.float32)
    hot_table = centred(keys[5], (HOT_ROWS, E), 1.0, 6.0)
    cold_table = centred(keys[6], (COLD_ROWS, E), 1.0, 6.0, ((0, 8),))
    first_weight = centred(keys[7], (H, F * F), (F * F) ** -0.5, 0.15625)
    second_weight = centred(keys[8], (H, H * F), (H * F) ** -0.5, 0.09375)
    third_weight = centred(keys[9], (H, H * F), (H * F) ** -0.5, 0.09375)
    out_weight = centred(keys[10], (3, H), (3 * H) ** -0.5, 0.375, (), jnp.float32)
    return dict(hot_row=hot_row, cold_row=cold_row, cold_owner=cold_owner, is_cold=is_cold, grad_logit=grad_logit, hot_table=hot_table, cold_table=cold_table, first_weight=first_weight, second_weight=second_weight, third_weight=third_weight, out_weight=out_weight)


def block_pass(embedded, grad_logit, layer_weights, out_weight):
    batch_rows, fields, breadth = embedded.shape
    base_wide = embedded.astype(jnp.float32)
    previous = embedded
    layer_inputs = []
    logit_sum = jnp.zeros((batch_rows,), jnp.float32)
    for section_index in range(len(layer_weights)):
        weight = layer_weights[section_index]
        below_maps = previous.shape[1]
        outer_rows = (previous.astype(jnp.float32)[:, :, None, :] * base_wide[:, None, :, :]).astype(jnp.bfloat16)
        outer_rows = outer_rows.reshape(batch_rows, below_maps * fields, breadth)
        current = jnp.einsum("hk,bke->bhe", weight.astype(jnp.float32), outer_rows.astype(jnp.float32)).astype(jnp.bfloat16)
        pooled = jnp.sum(current.astype(jnp.float32), axis=2)
        logit_sum = logit_sum + jnp.sum(pooled * out_weight[section_index][None, :], axis=1)
        layer_inputs.append(previous)
        previous = current
    grad_embedded = jnp.zeros((batch_rows, fields, breadth), jnp.float32)
    carried = jnp.zeros((batch_rows, out_weight.shape[1], breadth), jnp.float32)
    for section_index in reversed(range(len(layer_weights))):
        weight = layer_weights[section_index]
        lower_state = layer_inputs[section_index]
        below_maps = lower_state.shape[1]
        grad_state = carried + grad_logit[:, None, None] * out_weight[section_index][None, :, None]
        grad_low = grad_state.astype(jnp.bfloat16)
        grad_outer = jnp.einsum("hk,bhe->bke", weight.astype(jnp.float32), grad_low.astype(jnp.float32))
        grad_outer = grad_outer.reshape(batch_rows, below_maps, fields, breadth)
        grad_embedded = grad_embedded + jnp.sum(grad_outer * lower_state.astype(jnp.float32)[:, :, None, :], axis=1)
        carried = jnp.sum(grad_outer * base_wide[:, None, :, :], axis=2)
    grad_embedded = grad_embedded + carried
    return logit_sum, grad_embedded


def reference(hot_row, cold_row, cold_owner, is_cold, grad_logit, hot_table, cold_table, first_weight, second_weight, third_weight, out_weight):
    layer_weights = (first_weight, second_weight, third_weight)
    global_cold = (cold_owner * CR_DEV + cold_row).astype(jnp.int32)
    cold_flag = is_cold == 1
    embedded = jnp.where(cold_flag[:, :, None], jnp.take(cold_table, global_cold, axis=0), jnp.take(hot_table, hot_row, axis=0))
    blocks = SAMPLES // B_DEV
    embedded_blocks = embedded.reshape(blocks, B_DEV, F, E)
    grad_blocks = grad_logit.reshape(blocks, B_DEV)

    def one_block(block_pair):
        return block_pass(block_pair[0], block_pair[1], layer_weights, out_weight)

    logit_blocks, gradients = lax.map(one_block, (embedded_blocks, grad_blocks))
    gradients = gradients.reshape(SAMPLES * F, E)
    flag_flat = cold_flag.reshape(SAMPLES * F)
    hot_terms = jnp.where(flag_flat[:, None], 0.0, gradients)
    cold_terms = jnp.where(flag_flat[:, None], gradients, 0.0)
    hot_sum = jax.ops.segment_sum(hot_terms, hot_row.reshape(SAMPLES * F), num_segments=HOT_ROWS)
    cold_sum = jax.ops.segment_sum(cold_terms, global_cold.reshape(SAMPLES * F), num_segments=COLD_ROWS)
    return hot_sum.astype(jnp.bfloat16), cold_sum.astype(jnp.bfloat16), logit_blocks.reshape(SAMPLES)
```

```python
import functools

import jax
import jax.numpy as jnp
from jax import lax
from jax.experimental import pallas as pl
from jax.experimental.pallas import tpu as pltpu
from jax.sharding import PartitionSpec as P

BF = jnp.bfloat16
F32 = jnp.float32
MESH = pl.DeviceIdType.MESH
VMEM_LIMIT = 56 * 1024 * 1024


def up(value, unit):
    return (value + unit - 1) // unit * unit


def iota(shape, dim):
    return lax.broadcasted_iota(jnp.int32, shape, dim).astype(F32)


def dot(a, b):
    return jnp.dot(a, b, preferred_element_type=F32)


def dot_t(a, b):
    return lax.dot_general(a, b, (((0,), (0,)), ((), ())), preferred_element_type=F32)


def as_row(col, width):
    rows = col.shape[0]
    hit = iota((rows, width), 0) == iota((rows, width), 1)
    return jnp.sum(jnp.where(hit, col + 1.0, 0.0), axis=0, keepdims=True) - 1.0


def enter(me_g, me_s, n_g, n_s, groups):
    barrier = pltpu.get_barrier_semaphore()
    count = n_s - 1
    for k in range(1, n_s):
        pl.semaphore_signal(
            barrier, inc=1, device_id=(me_g, lax.rem(me_s + k, n_s)), device_id_type=MESH
        )
    if groups:
        count += n_g - 1
        for k in range(1, n_g):
            pl.semaphore_signal(
                barrier, inc=1, device_id=(lax.rem(me_g + k, n_g), me_s), device_id_type=MESH
            )
    pl.semaphore_wait(barrier, count)


def prepare_weight(w_ref, fields, maps_pad, fields_pad, wide, tall, wt_ref, wf_ref):
    high, cols = w_ref.shape
    cols_pad = up(cols, 128)
    total = fields_pad * maps_pad
    wide[...] = jnp.zeros_like(wide)
    wide[0:high, 0:cols] = w_ref[...].astype(F32)
    for b in range(cols_pad // 128):
        tall[b * 128 : (b + 1) * 128, :] = wide[:, b * 128 : (b + 1) * 128].T
    tall[cols_pad:, :] = jnp.zeros((tall.shape[0] - cols_pad, 128), F32)
    for f in range(fields_pad):
        block = slice(f * maps_pad, (f + 1) * maps_pad)
        if f < fields:
            wt_ref[block, :] = tall[pl.ds(f, maps_pad, stride=fields), :].astype(BF)
        else:
            wt_ref[block, :] = jnp.zeros((maps_pad, 128), BF)
    for b in range(total // 128):
        block = wt_ref[b * 128 : (b + 1) * 128, :].astype(F32).T
        wf_ref[:, b * 128 : (b + 1) * 128] = block[0 : wf_ref.shape[0]].astype(BF)


def lookup_kernel(
    n_g, n_s, cap,
    hot_row, cold_row, cold_owner, is_cold, hot_table, cold_table, w1, w2, w3, ow,
    emb, meta, wt1, wf1, wt2, wf2, wt3, wf3, owc,
    pack, wide, tall, ask, asked, reply, fetched, ask_s, ask_r, rep_s, rep_r,
):
    me_g, me_s = lax.axis_index("group"), lax.axis_index("shard")
    samples, fields = hot_row.shape
    fields_pad = up(fields, 8)
    looks = samples * fields_pad
    cap_pad = fetched.shape[1]
    slots = n_s * cap_pad
    hot_rows, shard_rows = hot_table.shape[0], cold_table.shape[0]

    pack[...] = jnp.full(pack.shape, -1.0, F32)
    for a, ref in enumerate((hot_row, cold_row, cold_owner, is_cold)):
        pack[a * samples : (a + 1) * samples, 0:fields] = ref[...].astype(F32)
    turned = pack[...].T

    def column(a):
        return jnp.concatenate(
            [
                turned[0:fields_pad, a * samples + s : a * samples + s + 1]
                for s in range(samples)
            ],
            axis=0,
        )

    hot_c, row_c, owner_c, flag_c = (column(a) for a in range(4))
    cold = flag_c == 1.0
    lanes = iota((looks, 128), 1)
    wanted = jnp.where(jnp.logical_and(owner_c == lanes, cold), 1.0, 0.0)
    lower = jnp.where(iota((looks, looks), 1) < iota((looks, looks), 0), 1.0, 0.0)
    earlier = dot(lower.astype(BF), wanted.astype(BF))
    pos_c = jnp.sum(earlier * wanted, axis=1, keepdims=True)
    target_c = jnp.where(cold, owner_c * cap_pad + pos_c, -1.0)
    at_pos = jnp.where(jnp.logical_and(pos_c == lanes, cold), 1.0, 0.0)
    code = row_c + 1.0
    code_hi = jnp.floor(code * (1.0 / 128.0))
    code_lo = code - code_hi * 128.0
    coded = jnp.concatenate([at_pos * code_hi, at_pos * code_lo], axis=1)
    found = dot_t(wanted.astype(BF), coded.astype(BF))
    ids = found[:, 0:128] * 128.0 + found[:, 128:256] - 1.0
    for o in range(n_s):
        ask[o] = jnp.broadcast_to(ids[o : o + 1, :], (8, 128))

    enter(me_g, me_s, n_g, n_s, False)

    def ask_copy(k):
        peer = lax.rem(me_s + k, n_s)
        return pltpu.make_async_remote_copy(
            src_ref=ask.at[peer], dst_ref=asked.at[me_s], send_sem=ask_s.at[k],
            recv_sem=ask_r.at[k], device_id=(me_g, peer), device_id_type=MESH,
        )

    def ask_wait(k):
        src = lax.rem(me_s + n_s - k, n_s)
        return pltpu.make_async_remote_copy(
            src_ref=ask.at[src], dst_ref=asked.at[src], send_sem=ask_s.at[k],
            recv_sem=ask_r.at[k], device_id=(me_g, src), device_id_type=MESH,
        )

    for k in range(1, n_s):
        ask_copy(k).start()
    asked[me_s] = ask[me_s]

    at_hot = jnp.logical_and(hot_c == iota((looks, hot_rows), 1), jnp.logical_not(cold))
    hot_part = dot(jnp.where(at_hot, 1.0, 0.0).astype(BF), hot_table[...])
    prepare_weight(w1, fields, wt1.shape[0] // fields_pad, fields_pad, wide, tall, wt1, wf1)

    for k in range(1, n_s):
        ask_wait(k).wait_recv()
    pack[...] = jnp.full(pack.shape, -1.0, F32)
    for d in range(n_s):
        pack[d : d + 1, :] = asked[d][0:1, :]
    turned2 = pack[...].T
    ids_c = jnp.concatenate([turned2[0:cap_pad, d : d + 1] for d in range(n_s)], axis=0)
    at_row = jnp.where(ids_c == iota((slots, shard_rows), 1), 1.0, 0.0)
    rows = dot(at_row.astype(BF), cold_table[...]).astype(BF)
    for d in range(n_s):
        reply[d] = rows[d * cap_pad : (d + 1) * cap_pad]

    def rep_copy(k):
        peer = lax.rem(me_s + k, n_s)
        return pltpu.make_async_remote_copy(
            src_ref=reply.at[peer], dst_ref=fetched.at[me_s], send_sem=rep_s.at[k],
            recv_sem=rep_r.at[k], device_id=(me_g, peer), device_id_type=MESH,
        )

    def rep_wait(k):
        src = lax.rem(me_s + n_s - k, n_s)
        return pltpu.make_async_remote_copy(
            src_ref=reply.at[src], dst_ref=fetched.at[src], send_sem=rep_s.at[k],
            recv_sem=rep_r.at[k], device_id=(me_g, src), device_id_type=MESH,
        )

    for k in range(1, n_s):
        rep_copy(k).start()
    fetched[me_s] = reply[me_s]

    prepare_weight(w2, fields, wt2.shape[0] // fields_pad, fields_pad, wide, tall, wt2, wf2)
    prepare_weight(w3, fields, wt3.shape[0] // fields_pad, fields_pad, wide, tall, wt3, wf3)
    width = meta.shape[1]
    meta[...] = jnp.full(meta.shape, -1.0, F32)
    meta[0:1, :] = as_row(jnp.where(cold, -1.0, hot_c), width)
    meta[1:2, :] = as_row(target_c, width)
    meta[2:3, :] = as_row(ids_c, width)
    pack[...] = jnp.zeros(pack.shape, F32)
    pack[0 : ow.shape[0], 0 : ow.shape[1]] = ow[...]
    owc[...] = pack[...].T

    for k in range(1, n_s):
        rep_wait(k).wait_recv()
    at_slot = jnp.where(target_c == iota((looks, slots), 1), 1.0, 0.0).astype(BF)
    got = jnp.concatenate([fetched[d] for d in range(n_s)], axis=0)
    emb[...] = (dot(at_slot, got) + hot_part).astype(BF)
    for k in range(1, n_s):
        ask_copy(k).wait_send()
        rep_copy(k).wait_send()


def layers_kernel(
    fields, gl, emb, wt1, wf1, wt2, wf2, wt3, wf3, owc,
    grad, logit, outer, base, low, states, ge,
):
    fields_pad = base.shape[0]
    samples = emb.shape[0] // fields_pad
    pair = base.shape[1] // 128
    high = wf1.shape[0]
    wts, wfs = (wt1, wt2, wt3), (wf1, wf2, wf3)

    @pl.loop(0, samples // pair)
    def _(b):
        row0 = pl.multiple_of(b * (pair * fields_pad), 8)
        block = emb[pl.ds(row0, pair * fields_pad), :].astype(F32)
        x0 = jnp.concatenate(
            [block[p * fields_pad : (p + 1) * fields_pad] for p in range(pair)], axis=1
        )
        base[...] = x0
        lanes = base.shape[1]
        grow = jnp.concatenate(
            [jnp.full((1, 128), gl[b * pair + p], F32) for p in range(pair)], axis=1
        )
        first_pad = wt1.shape[0] // fields_pad
        low[0:fields_pad, :] = x0
        low[fields_pad:first_pad, :] = jnp.zeros((first_pad - fields_pad, lanes), F32)
        below = low[...]
        inputs = [below]
        total = jnp.zeros((1, lanes), F32)
        for k in range(3):
            maps_pad = wts[k].shape[0] // fields_pad
            below_b = below.astype(BF)
            for f in range(fields_pad):
                start = f * maps_pad
                if f < fields:
                    wide = jnp.broadcast_to(base[f : f + 1, :], (16, lanes)).astype(BF)
                    for t in range(maps_pad // 16):
                        outer[start + t * 16 : start + t * 16 + 16, :] = (
                            below_b[t * 16 : t * 16 + 16] * wide
                        )
                else:
                    outer[start : start + maps_pad, :] = jnp.zeros((maps_pad, lanes), BF)
            depth = fields_pad * maps_pad
            state = dot(wfs[k][...], outer[0:depth, :]).astype(BF).astype(F32)
            total = total + jnp.sum(state * owc[0:high, k : k + 1], axis=0, keepdims=True)
            states[k] = state
            below = state
        for p in range(pair):
            one = jnp.sum(total[:, p * 128 : (p + 1) * 128], axis=1, keepdims=True)
            logit[pl.ds(b * pair + p, 1), :] = jnp.broadcast_to(one, (1, 128))

        carried = jnp.zeros((high, lanes), F32)
        chunk = 8
        for k in (2, 1, 0):
            maps_pad = wts[k].shape[0] // fields_pad
            used = maps_pad - 8
            grad_state = carried + owc[0:high, k : k + 1] * grow
            grad_low = jnp.concatenate(
                [grad_state.astype(BF), jnp.zeros((128 - high, lanes), BF)], axis=0
            )
            lower = low if k == 0 else states.at[k - 1]
            acc = jnp.zeros((used, lanes), F32)
            for c in range(0, fields, chunk):
                many = min(chunk, fields_pad - c)
                g = dot(wts[k][c * maps_pad : (c + many) * maps_pad, :], grad_low)
                for f in range(c, min(c + many, fields)):
                    gf = g[(f - c) * maps_pad : (f - c) * maps_pad + used]
                    acc = acc + gf * base[f : f + 1, :]
                    part = jnp.sum(gf * lower[0:used, :], axis=0, keepdims=True)
                    if k == 2:
                        ge[f : f + 1, :] = part
                    else:
                        ge[f : f + 1, :] += part
            if k > 0:
                carried = jnp.concatenate(
                    [acc, jnp.zeros((high - used, lanes), F32)], axis=0
                )
            else:
                carried = acc
        out = ge[...] + carried[0:fields_pad]
        keep = lax.broadcasted_iota(jnp.int32, out.shape, 0) < fields
        out = jnp.where(keep, out, 0.0).astype(BF)
        grad[pl.ds(row0, pair * fields_pad), :] = jnp.concatenate(
            [out[:, p * 128 : (p + 1) * 128] for p in range(pair)], axis=0
        )


def grads_kernel(
    n_g, n_s, cap_pad, grad, meta,
    hot_out, cold_out,
    send, inc, allin, ids, hot_part, hot_in, hot_mid, hot_all,
    send_s, send_r, all_s, all_r, id_s, id_r, hs_s, hs_r, hm_s, hm_r, hg_s, hg_r,
):
    me_g, me_s = lax.axis_index("group"), lax.axis_index("shard")
    looks = grad.shape[0]
    slots = n_s * cap_pad
    hot_rows, shard_rows = hot_out.shape[0], cold_out.shape[0]
    part = hot_rows // n_s

    def shard_copy(k, src, dst, s_sem, r_sem):
        peer = lax.rem(me_s + k, n_s)
        return pltpu.make_async_remote_copy(
            src_ref=src(peer), dst_ref=dst(me_s), send_sem=s_sem.at[k],
            recv_sem=r_sem.at[k], device_id=(me_g, peer), device_id_type=MESH,
        )

    def shard_wait(k, src, dst, s_sem, r_sem):
        peer = lax.rem(me_s + n_s - k, n_s)
        return pltpu.make_async_remote_copy(
            src_ref=src(peer), dst_ref=dst(peer), send_sem=s_sem.at[k],
            recv_sem=r_sem.at[k], device_id=(me_g, peer), device_id_type=MESH,
        )

    def group_copy(k, src, dst, s_sem, r_sem):
        peer = lax.rem(me_g + k, n_g)
        return pltpu.make_async_remote_copy(
            src_ref=src, dst_ref=dst(me_g), send_sem=s_sem.at[k],
            recv_sem=r_sem.at[k], device_id=(peer, me_s), device_id_type=MESH,
        )

    def group_wait(k, src, dst, s_sem, r_sem):
        peer = lax.rem(me_g + n_g - k, n_g)
        return pltpu.make_async_remote_copy(
            src_ref=src, dst_ref=dst(peer), send_sem=s_sem.at[k],
            recv_sem=r_sem.at[k], device_id=(peer, me_s), device_id_type=MESH,
        )

    cold_x = (lambda p: send.at[p], lambda p: inc.at[p], send_s, send_r)
    cold_g = (inc, lambda p: allin.at[p], all_s, all_r)
    id_g = (meta, lambda p: ids.at[p], id_s, id_r)
    hot_x = (lambda p: hot_part.at[p], lambda p: hot_in.at[p], hs_s, hs_r)
    hot_g = (hot_mid, lambda p: hot_all.at[p], hm_s, hm_r)

    def hot_slice(p):
        return hot_out.at[pl.ds(pl.multiple_of(p * part, part), part)]

    hot_f = (lambda p: hot_slice(me_s), hot_slice, hg_s, hg_r)

    g = grad[...]
    at_slot = jnp.where(meta[1:2, 0:looks] == iota((slots, looks), 0), 1.0, 0.0)
    out = dot(at_slot.astype(BF), g).astype(BF)
    for d in range(n_s):
        send[d] = out[d * cap_pad : (d + 1) * cap_pad]

    enter(me_g, me_s, n_g, n_s, True)
    for k in range(1, n_s):
        shard_copy(k, *cold_x).start()
    for k in range(1, n_g):
        group_copy(k, *id_g).start()
    inc[me_s] = send[me_s]
    ids[me_g] = meta[...]

    at_hot = jnp.where(meta[0:1, 0:looks] == iota((hot_rows, looks), 0), 1.0, 0.0)
    hots = dot(at_hot.astype(BF), g).astype(BF)
    for d in range(n_s):
        hot_part[d] = hots[d * part : (d + 1) * part]
    for k in range(1, n_s):
        shard_copy(k, *hot_x).start()
    hot_in[me_s] = hot_part[me_s]

    for k in range(1, n_s):
        shard_wait(k, *cold_x).wait_recv()
    for k in range(1, n_g):
        group_copy(k, *cold_g).start()
    allin[me_g] = inc[...]

    for k in range(1, n_s):
        shard_wait(k, *hot_x).wait_recv()
    total = hot_in[0].astype(F32)
    for d in range(1, n_s):
        total = total + hot_in[d].astype(F32)
    hot_mid[...] = total.astype(BF)
    for k in range(1, n_g):
        group_copy(k, *hot_g).start()
    hot_all[me_g] = hot_mid[...]

    for k in range(1, n_g):
        group_wait(k, *hot_g).wait_recv()
    total = hot_all[0].astype(F32)
    for d in range(1, n_g):
        total = total + hot_all[d].astype(F32)
    hot_slice(me_s)[...] = total.astype(BF)
    for k in range(1, n_s):
        shard_copy(k, *hot_f).start()

    for k in range(1, n_g):
        group_wait(k, *id_g).wait_recv()
        group_wait(k, *cold_g).wait_recv()
    terms = jnp.concatenate(
        [allin[q, d] for q in range(n_g) for d in range(n_s)], axis=0
    )
    step = 512 if shard_rows % 512 == 0 else shard_rows

    @pl.loop(0, shard_rows // step)
    def _(t):
        first = pl.multiple_of(t * step, step)
        here = iota((step, slots), 0) + first.astype(F32)
        at = jnp.concatenate(
            [
                jnp.where(ids[q][2:3, 0:slots] == here, 1.0, 0.0).astype(BF)
                for q in range(n_g)
            ],
            axis=1,
        )
        cold_out[pl.ds(first, step), :] = dot(at, terms).astype(BF)

    for k in range(1, n_s):
        shard_wait(k, *hot_f).wait_recv()
    for k in range(1, n_s):
        shard_copy(k, *cold_x).wait_send()
        shard_copy(k, *hot_x).wait_send()
        shard_copy(k, *hot_f).wait_send()
    for k in range(1, n_g):
        group_copy(k, *id_g).wait_send()
        group_copy(k, *cold_g).wait_send()
        group_copy(k, *hot_g).wait_send()


def local(
    hot_row, cold_row, cold_owner, is_cold, grad_logit, hot_table, cold_table,
    first_weight, second_weight, third_weight, out_weight,
):
    n_g, n_s = lax.axis_size("group"), lax.axis_size("shard")
    samples, fields = hot_row.shape
    breadth = hot_table.shape[1]
    maps = out_weight.shape[1]
    cap = samples * fields // n_s
    cap_pad = up(cap, 16)
    slots = n_s * cap_pad
    fields_pad = up(fields, 8)
    looks = samples * fields_pad
    first_pad, maps_pad = up(fields_pad, 16), up(maps, 16)
    depth1, depth2 = fields_pad * first_pad, fields_pad * maps_pad
    wide = up(max(slots, looks), 128)
    vm = pl.BlockSpec(memory_space=pltpu.VMEM)
    sd = jax.ShapeDtypeStruct
    dma = pltpu.SemaphoreType.DMA

    emb, meta, wt1, wf1, wt2, wf2, wt3, wf3, owc = pl.pallas_call(
        functools.partial(lookup_kernel, n_g, n_s, cap),
        out_shape=(
            sd((looks, breadth), BF), sd((8, wide), F32),
            sd((depth1, 128), BF), sd((maps_pad, depth1), BF),
            sd((depth2, 128), BF), sd((maps_pad, depth2), BF),
            sd((depth2, 128), BF), sd((maps_pad, depth2), BF),
            sd((128, 128), F32),
        ),
        in_specs=[vm] * 10,
        out_specs=tuple([vm] * 9),
        scratch_shapes=[
            pltpu.VMEM((128, 128), F32),
            pltpu.VMEM((128, up(second_weight.shape[1], 128)), F32),
            pltpu.VMEM((depth2, 128), F32),
            pltpu.VMEM((n_s, 8, 128), F32),
            pltpu.VMEM((n_s, 8, 128), F32),
            pltpu.VMEM((n_s, cap_pad, breadth), BF),
            pltpu.VMEM((n_s, cap_pad, breadth), BF),
            dma((n_s,)), dma((n_s,)), dma((n_s,)), dma((n_s,)),
        ],
        compiler_params=pltpu.CompilerParams(
            collective_id=0, has_side_effects=True, vmem_limit_bytes=VMEM_LIMIT
        ),
        name="lookup",
    )(
        hot_row, cold_row, cold_owner, is_cold, hot_table, cold_table,
        first_weight, second_weight, third_weight, out_weight,
    )

    pair = 2
    lanes = pair * 128
    grad, logit = pl.pallas_call(
        functools.partial(layers_kernel, fields),
        out_shape=(sd((looks, breadth), BF), sd((samples, 128), F32)),
        in_specs=[pl.BlockSpec(memory_space=pltpu.SMEM)] + [vm] * 8,
        out_specs=(vm, vm),
        scratch_shapes=[
            pltpu.VMEM((depth2, lanes), BF),
            pltpu.VMEM((fields_pad, lanes), F32),
            pltpu.VMEM((first_pad, lanes), F32),
            pltpu.VMEM((3, maps_pad, lanes), F32),
            pltpu.VMEM((fields_pad, lanes), F32),
        ],
        compiler_params=pltpu.CompilerParams(vmem_limit_bytes=VMEM_LIMIT),
        name="layers",
    )(grad_logit, emb, wt1, wf1, wt2, wf2, wt3, wf3, owc)

    part = hot_table.shape[0] // n_s
    hot_grad, cold_grad = pl.pallas_call(
        functools.partial(grads_kernel, n_g, n_s, cap_pad),
        out_shape=(sd(hot_table.shape, BF), sd(cold_table.shape, BF)),
        in_specs=[vm, vm],
        out_specs=(vm, vm),
        scratch_shapes=[
            pltpu.VMEM((n_s, cap_pad, breadth), BF),
            pltpu.VMEM((n_s, cap_pad, breadth), BF),
            pltpu.VMEM((n_g, n_s, cap_pad, breadth), BF),
            pltpu.VMEM((n_g, 8, wide), F32),
            pltpu.VMEM((n_s, part, breadth), BF),
            pltpu.VMEM((n_s, part, breadth), BF),
            pltpu.VMEM((part, breadth), BF),
            pltpu.VMEM((n_g, part, breadth), BF),
            dma((n_s,)), dma((n_s,)), dma((n_g,)), dma((n_g,)), dma((n_g,)), dma((n_g,)),
            dma((n_s,)), dma((n_s,)), dma((n_g,)), dma((n_g,)), dma((n_s,)), dma((n_s,)),
        ],
        compiler_params=pltpu.CompilerParams(
            collective_id=1, has_side_effects=True, vmem_limit_bytes=VMEM_LIMIT
        ),
        name="grads",
    )(grad, meta)
    return hot_grad, cold_grad, logit[:, 0]


def solution(mesh):
    rows = P(("group", "shard"), None)
    return jax.shard_map(
        local,
        mesh=mesh,
        in_specs=(
            rows, rows, rows, rows, P(("group", "shard")), P(), P("shard", None),
            P(), P(), P(), P(),
        ),
        out_specs=(P(), P("shard", None), P(("group", "shard"))),
        check_vma=False,
    )
```

```python
import functools

import jax
import jax.numpy as jnp
from jax import lax
from jax.experimental import pallas as pl
from jax.experimental.pallas import tpu as pltpu
from jax.sharding import PartitionSpec as P

BF = jnp.bfloat16
F32 = jnp.float32
MESH = pl.DeviceIdType.MESH
VMEM_LIMIT = 56 * 1024 * 1024


def up(value, unit):
    return (value + unit - 1) // unit * unit


def iota(shape, dim):
    return lax.broadcasted_iota(jnp.int32, shape, dim).astype(F32)


def dot(a, b):
    return jnp.dot(a, b, preferred_element_type=F32)


def dot_t(a, b):
    return lax.dot_general(a, b, (((0,), (0,)), ((), ())), preferred_element_type=F32)


def as_row(col, width):
    rows = col.shape[0]
    hit = iota((rows, width), 0) == iota((rows, width), 1)
    return jnp.sum(jnp.where(hit, col + 1.0, 0.0), axis=0, keepdims=True) - 1.0


def prepare_weight(w_ref, fields, maps_pad, fields_pad, wide, tall, wt_ref, wf_ref):
    high, cols = w_ref.shape
    cols_pad = up(cols, 128)
    total = fields_pad * maps_pad
    wide[...] = jnp.zeros_like(wide)
    wide[0:high, 0:cols] = w_ref[...].astype(F32)
    for b in range(cols_pad // 128):
        tall[b * 128 : (b + 1) * 128, :] = wide[:, b * 128 : (b + 1) * 128].T
    tall[cols_pad:, :] = jnp.zeros((tall.shape[0] - cols_pad, 128), F32)
    for f in range(fields_pad):
        block = slice(f * maps_pad, (f + 1) * maps_pad)
        if f < fields:
            wt_ref[block, :] = tall[pl.ds(f, maps_pad, stride=fields), :].astype(BF)
        else:
            wt_ref[block, :] = jnp.zeros((maps_pad, 128), BF)
    for b in range(total // 128):
        block = wt_ref[b * 128 : (b + 1) * 128, :].astype(F32).T
        wf_ref[:, b * 128 : (b + 1) * 128] = block[0 : wf_ref.shape[0]].astype(BF)


def step_kernel(
    n_g, n_s,
    hot_row, cold_row, cold_owner, is_cold, gl, hot_table, cold_table, w1, w2, w3, ow,
    hot_out, cold_out, logit,
    hot_v, cold_v, w1_v, w2_v, w3_v, emb, wt1, wf1, wt2, wf2, wt3, wf3, owc, meta,
    pack, wide, tall, ask, asked, reply, fetched,
    outer, base, low, states, ge,
    gmine, gall, inc, allin, ids_all, hot_mid, hot_all,
    load_s, ask_s, ask_r, rep_s, rep_r, sp_s, sp_r,
    all_s, all_r, id_s, id_r, hm_s, hm_r, hg_s, hg_r,
):
    me_g, me_s = lax.axis_index("group"), lax.axis_index("shard")
    barrier = pltpu.get_barrier_semaphore()
    for k in range(1, n_s):
        pl.semaphore_signal(
            barrier, inc=1, device_id=(me_g, lax.rem(me_s + k, n_s)), device_id_type=MESH
        )
    for k in range(1, n_g):
        pl.semaphore_signal(
            barrier, inc=1, device_id=(lax.rem(me_g + k, n_g), me_s), device_id_type=MESH
        )
    loads = [
        pltpu.make_async_copy(src, dst, load_s.at[i])
        for i, (src, dst) in enumerate(
            ((hot_table, hot_v), (cold_table, cold_v), (w1, w1_v), (w2, w2_v), (w3, w3_v))
        )
    ]
    for load in loads:
        load.start()
    samples, fields = hot_row.shape
    fields_pad = up(fields, 8)
    looks = samples * fields_pad
    cap_pad = fetched.shape[1]
    slots = n_s * cap_pad
    hot_rows, shard_rows = hot_out.shape[0], cold_out.shape[0]
    part = hot_rows // n_s
    pair = base.shape[1] // 128
    high = wf1.shape[0]
    wts, wfs = (wt1, wt2, wt3), (wf1, wf2, wf3)

    def shard_copy(k, src, dst, s_sem, r_sem):
        peer = lax.rem(me_s + k, n_s)
        return pltpu.make_async_remote_copy(
            src_ref=src(peer), dst_ref=dst(me_s), send_sem=s_sem.at[k],
            recv_sem=r_sem.at[k], device_id=(me_g, peer), device_id_type=MESH,
        )

    def shard_wait(k, src, dst, s_sem, r_sem):
        peer = lax.rem(me_s + n_s - k, n_s)
        return pltpu.make_async_remote_copy(
            src_ref=src(peer), dst_ref=dst(peer), send_sem=s_sem.at[k],
            recv_sem=r_sem.at[k], device_id=(me_g, peer), device_id_type=MESH,
        )

    def group_copy(k, src, dst, s_sem, r_sem):
        peer = lax.rem(me_g + k, n_g)
        return pltpu.make_async_remote_copy(
            src_ref=src, dst_ref=dst(me_g), send_sem=s_sem.at[k],
            recv_sem=r_sem.at[k], device_id=(peer, me_s), device_id_type=MESH,
        )

    def group_wait(k, src, dst, s_sem, r_sem):
        peer = lax.rem(me_g + n_g - k, n_g)
        return pltpu.make_async_remote_copy(
            src_ref=src, dst_ref=dst(peer), send_sem=s_sem.at[k],
            recv_sem=r_sem.at[k], device_id=(peer, me_s), device_id_type=MESH,
        )

    cold_g = (inc, lambda p: allin.at[p], all_s, all_r)
    id_g = (meta, lambda p: ids_all.at[p], id_s, id_r)
    hot_g = (hot_mid, lambda p: hot_all.at[p], hm_s, hm_r)

    def hot_slice(p):
        return hot_out.at[pl.ds(pl.multiple_of(p * part, part), part)]

    hot_f = (lambda p: hot_slice(me_s), hot_slice, hg_s, hg_r)

    def spread_copy(b, k):
        peer = lax.rem(me_s + k, n_s)
        return pltpu.make_async_remote_copy(
            src_ref=gmine.at[b], dst_ref=gall.at[me_s, b], send_sem=sp_s.at[b, k],
            recv_sem=sp_r.at[b, k], device_id=(me_g, peer), device_id_type=MESH,
        )

    def spread_wait(b, k):
        src = lax.rem(me_s + n_s - k, n_s)
        return pltpu.make_async_remote_copy(
            src_ref=gmine.at[b], dst_ref=gall.at[src, b], send_sem=sp_s.at[b, k],
            recv_sem=sp_r.at[b, k], device_id=(me_g, src), device_id_type=MESH,
        )

    pack[...] = jnp.full(pack.shape, -1.0, F32)
    for a, ref in enumerate((hot_row, cold_row, cold_owner, is_cold)):
        pack[a * samples : (a + 1) * samples, 0:fields] = ref[...].astype(F32)
    turned = pack[...].T

    def column(a):
        return jnp.concatenate(
            [
                turned[0:fields_pad, a * samples + s : a * samples + s + 1]
                for s in range(samples)
            ],
            axis=0,
        )

    hot_c, row_c, owner_c, flag_c = (column(a) for a in range(4))
    cold = flag_c == 1.0
    lanes = iota((looks, 128), 1)
    wanted = jnp.where(jnp.logical_and(owner_c == lanes, cold), 1.0, 0.0)
    lower = jnp.where(iota((looks, looks), 1) < iota((looks, looks), 0), 1.0, 0.0)
    earlier = dot(lower.astype(BF), wanted.astype(BF))
    pos_c = jnp.sum(earlier * wanted, axis=1, keepdims=True)
    target_c = jnp.where(cold, owner_c * cap_pad + pos_c, -1.0)
    at_pos = jnp.where(jnp.logical_and(pos_c == lanes, cold), 1.0, 0.0)
    code = row_c + 1.0
    code_hi = jnp.floor(code * (1.0 / 128.0))
    code_lo = code - code_hi * 128.0
    coded = jnp.concatenate([at_pos * code_hi, at_pos * code_lo], axis=1)
    found = dot_t(wanted.astype(BF), coded.astype(BF))
    ids = found[:, 0:128] * 128.0 + found[:, 128:256] - 1.0
    width = meta.shape[1]
    hot_r = as_row(jnp.where(cold, -1.0, hot_c), width)
    target_r = as_row(target_c, width)
    for o in range(n_s):
        ask[o, 0:1, 0:128] = ids[o : o + 1, :]
        ask[o, 1:2, :] = hot_r
        ask[o, 2:3, :] = target_r

    pl.semaphore_wait(barrier, n_s - 1 + n_g - 1)

    def ask_copy(k):
        peer = lax.rem(me_s + k, n_s)
        return pltpu.make_async_remote_copy(
            src_ref=ask.at[peer], dst_ref=asked.at[me_s], send_sem=ask_s.at[k],
            recv_sem=ask_r.at[k], device_id=(me_g, peer), device_id_type=MESH,
        )

    def ask_wait(k):
        src = lax.rem(me_s + n_s - k, n_s)
        return pltpu.make_async_remote_copy(
            src_ref=ask.at[src], dst_ref=asked.at[src], send_sem=ask_s.at[k],
            recv_sem=ask_r.at[k], device_id=(me_g, src), device_id_type=MESH,
        )

    for k in range(1, n_s):
        ask_copy(k).start()
    asked[me_s] = ask[me_s]

    loads[0].wait()
    at_hot = jnp.logical_and(hot_c == iota((looks, hot_rows), 1), jnp.logical_not(cold))
    hot_part = dot(jnp.where(at_hot, 1.0, 0.0).astype(BF), hot_v[...])
    loads[2].wait()
    prepare_weight(w1_v, fields, wt1.shape[0] // fields_pad, fields_pad, wide, tall, wt1, wf1)

    for k in range(1, n_s):
        ask_wait(k).wait_recv()
    pack[...] = jnp.full(pack.shape, -1.0, F32)
    for d in range(n_s):
        pack[d : d + 1, :] = asked[d, 0:1, 0:128]
    turned2 = pack[...].T
    ids_c = jnp.concatenate([turned2[0:cap_pad, d : d + 1] for d in range(n_s)], axis=0)
    at_row = jnp.where(ids_c == iota((slots, shard_rows), 1), 1.0, 0.0)
    loads[1].wait()
    rows = dot(at_row.astype(BF), cold_v[...]).astype(BF)
    for d in range(n_s):
        reply[d] = rows[d * cap_pad : (d + 1) * cap_pad]

    def rep_copy(k):
        peer = lax.rem(me_s + k, n_s)
        return pltpu.make_async_remote_copy(
            src_ref=reply.at[peer], dst_ref=fetched.at[me_s], send_sem=rep_s.at[k],
            recv_sem=rep_r.at[k], device_id=(me_g, peer), device_id_type=MESH,
        )

    def rep_wait(k):
        src = lax.rem(me_s + n_s - k, n_s)
        return pltpu.make_async_remote_copy(
            src_ref=reply.at[src], dst_ref=fetched.at[src], send_sem=rep_s.at[k],
            recv_sem=rep_r.at[k], device_id=(me_g, src), device_id_type=MESH,
        )

    for k in range(1, n_s):
        rep_copy(k).start()
    fetched[me_s] = reply[me_s]

    meta[...] = jnp.broadcast_to(as_row(ids_c, width), meta.shape)
    for k in range(1, n_g):
        group_copy(k, *id_g).start()
    ids_all[me_g] = meta[...]
    loads[3].wait()
    prepare_weight(w2_v, fields, wt2.shape[0] // fields_pad, fields_pad, wide, tall, wt2, wf2)
    loads[4].wait()
    prepare_weight(w3_v, fields, wt3.shape[0] // fields_pad, fields_pad, wide, tall, wt3, wf3)
    pack[...] = jnp.zeros(pack.shape, F32)
    pack[0 : ow.shape[0], 0 : ow.shape[1]] = ow[...]
    owc[...] = pack[...].T

    for k in range(1, n_s):
        rep_wait(k).wait_recv()
    at_slot = jnp.where(target_c == iota((looks, slots), 1), 1.0, 0.0).astype(BF)
    got = jnp.concatenate([fetched[d] for d in range(n_s)], axis=0)
    emb[...] = (dot(at_slot, got) + hot_part).astype(BF)
    for k in range(1, n_s):
        ask_copy(k).wait_send()
        rep_copy(k).wait_send()

    @pl.loop(0, samples // pair)
    def _(b):
        row0 = pl.multiple_of(b * (pair * fields_pad), 8)
        block = emb[pl.ds(row0, pair * fields_pad), :].astype(F32)
        x0 = jnp.concatenate(
            [block[p * fields_pad : (p + 1) * fields_pad] for p in range(pair)], axis=1
        )
        base[...] = x0
        lanes = base.shape[1]
        grow = jnp.concatenate(
            [jnp.full((1, 128), gl[b * pair + p], F32) for p in range(pair)], axis=1
        )
        first_pad = wt1.shape[0] // fields_pad
        low[0:fields_pad, :] = x0
        low[fields_pad:first_pad, :] = jnp.zeros((first_pad - fields_pad, lanes), F32)
        below = low[...]
        inputs = [below]
        total = jnp.zeros((1, lanes), F32)
        for k in range(3):
            maps_pad = wts[k].shape[0] // fields_pad
            below_b = below.astype(BF)
            for f in range(fields_pad):
                start = f * maps_pad
                if f < fields:
                    wide = jnp.broadcast_to(base[f : f + 1, :], (16, lanes)).astype(BF)
                    for t in range(maps_pad // 16):
                        outer[start + t * 16 : start + t * 16 + 16, :] = (
                            below_b[t * 16 : t * 16 + 16] * wide
                        )
                else:
                    outer[start : start + maps_pad, :] = jnp.zeros((maps_pad, lanes), BF)
            depth = fields_pad * maps_pad
            state = dot(wfs[k][...], outer[0:depth, :]).astype(BF).astype(F32)
            total = total + jnp.sum(state * owc[0:high, k : k + 1], axis=0, keepdims=True)
            states[k] = state
            below = state
        for p in range(pair):
            logit[b * pair + p] = jnp.sum(total[:, p * 128 : (p + 1) * 128])

        carried = jnp.zeros((high, lanes), F32)
        chunk = 8
        for k in (2, 1, 0):
            maps_pad = wts[k].shape[0] // fields_pad
            used = fields_pad if k == 0 else up(ow.shape[1], 8)
            grad_state = carried + owc[0:high, k : k + 1] * grow
            grad_low = jnp.concatenate(
                [grad_state.astype(BF), jnp.zeros((128 - high, lanes), BF)], axis=0
            )
            lower = low if k == 0 else states.at[k - 1]
            acc = jnp.zeros((used, lanes), F32)
            for c in range(0, fields, chunk):
                many = min(chunk, fields_pad - c)
                g = dot(wts[k][c * maps_pad : (c + many) * maps_pad, :], grad_low)
                for f in range(c, min(c + many, fields)):
                    gf = g[(f - c) * maps_pad : (f - c) * maps_pad + used]
                    acc = acc + gf * base[f : f + 1, :]
                    part = jnp.sum(gf * lower[0:used, :], axis=0, keepdims=True)
                    if k == 2:
                        ge[f : f + 1, :] = part
                    else:
                        ge[f : f + 1, :] += part
            if k > 0:
                carried = jnp.concatenate(
                    [acc, jnp.zeros((high - used, lanes), F32)], axis=0
                )
            else:
                carried = acc
        out = ge[...] + carried[0:fields_pad]
        keep = lax.broadcasted_iota(jnp.int32, out.shape, 0) < fields
        out = jnp.where(keep, out, 0.0).astype(BF)
        gmine[b] = jnp.concatenate(
            [out[:, p * 128 : (p + 1) * 128] for p in range(pair)], axis=0
        )
        for k in range(1, n_s):
            spread_copy(b, k).start()
        gall[me_s, b] = gmine[b]

    blocks = gmine.shape[0]
    for b in range(blocks):
        for k in range(1, n_s):
            spread_wait(b, k).wait_recv()
    mine = (me_s * part).astype(F32)
    first_slot = (me_s * cap_pad).astype(F32)
    hot_sum = jnp.zeros((part, 128), F32)
    for d in range(n_s):
        terms = jnp.concatenate([gall[d, b] for b in range(blocks)], axis=0)
        hot_r = asked[d, 1:2, 0:looks] - mine
        slot_r = asked[d, 2:3, 0:looks] - first_slot
        at = jnp.concatenate(
            [
                jnp.where(hot_r == iota((part, looks), 0), 1.0, 0.0),
                jnp.where(slot_r == iota((cap_pad, looks), 0), 1.0, 0.0),
            ],
            axis=0,
        )
        both = dot(at.astype(BF), terms)
        hot_sum = hot_sum + both[0:part]
        inc[d] = both[part : part + cap_pad].astype(BF)
    hot_mid[...] = hot_sum.astype(BF)
    for k in range(1, n_g):
        group_copy(k, *hot_g).start()
    for k in range(1, n_g):
        group_copy(k, *cold_g).start()
    hot_all[me_g] = hot_mid[...]
    allin[me_g] = inc[...]

    for k in range(1, n_g):
        group_wait(k, *hot_g).wait_recv()
    total = hot_all[0].astype(F32)
    for d in range(1, n_g):
        total = total + hot_all[d].astype(F32)
    hot_slice(me_s)[...] = total.astype(BF)
    for k in range(1, n_s):
        shard_copy(k, *hot_f).start()

    for k in range(1, n_g):
        group_wait(k, *id_g).wait_recv()
        group_wait(k, *cold_g).wait_recv()
    terms = jnp.concatenate(
        [allin[q, d] for q in range(n_g) for d in range(n_s)], axis=0
    )
    step = 512 if shard_rows % 512 == 0 else shard_rows

    @pl.loop(0, shard_rows // step)
    def _(t):
        first = pl.multiple_of(t * step, step)
        here = iota((step, slots), 0) + first.astype(F32)
        at = jnp.concatenate(
            [
                jnp.where(ids_all[q][0:1, 0:slots] == here, 1.0, 0.0).astype(BF)
                for q in range(n_g)
            ],
            axis=1,
        )
        cold_out[pl.ds(first, step), :] = dot(at, terms).astype(BF)

    for k in range(1, n_s):
        shard_wait(k, *hot_f).wait_recv()
    for k in range(1, n_s):
        for b in range(blocks):
            spread_copy(b, k).wait_send()
        shard_copy(k, *hot_f).wait_send()
    for k in range(1, n_g):
        group_copy(k, *id_g).wait_send()
        group_copy(k, *cold_g).wait_send()
        group_copy(k, *hot_g).wait_send()


def local(
    hot_row, cold_row, cold_owner, is_cold, grad_logit, hot_table, cold_table,
    first_weight, second_weight, third_weight, out_weight,
):
    n_g, n_s = lax.axis_size("group"), lax.axis_size("shard")
    samples, fields = hot_row.shape
    breadth = hot_table.shape[1]
    maps = out_weight.shape[1]
    cap_pad = up(samples * fields // n_s, 16)
    slots = n_s * cap_pad
    fields_pad = up(fields, 8)
    looks = samples * fields_pad
    first_pad, maps_pad = up(fields_pad, 16), up(maps, 16)
    depth1, depth2 = fields_pad * first_pad, fields_pad * maps_pad
    wide = up(max(slots, looks), 128)
    pair = 2
    lanes = pair * 128
    blocks = samples // pair
    part = hot_table.shape[0] // n_s
    vm = pl.BlockSpec(memory_space=pltpu.VMEM)
    sm = pl.BlockSpec(memory_space=pltpu.SMEM)
    hbm = pl.BlockSpec(memory_space=pl.ANY)
    sd = jax.ShapeDtypeStruct
    dma = pltpu.SemaphoreType.DMA
    V = pltpu.VMEM
    return pl.pallas_call(
        functools.partial(step_kernel, n_g, n_s),
        out_shape=(
            sd(hot_table.shape, BF), sd(cold_table.shape, BF), sd((samples,), F32)
        ),
        in_specs=[vm] * 4 + [sm] + [hbm] * 5 + [vm],
        out_specs=(vm, vm, sm),
        scratch_shapes=[
            V(hot_table.shape, BF), V(cold_table.shape, BF), V(first_weight.shape, BF),
            V(second_weight.shape, BF), V(third_weight.shape, BF),
            V((looks, breadth), BF),
            V((depth1, 128), BF), V((maps_pad, depth1), BF),
            V((depth2, 128), BF), V((maps_pad, depth2), BF),
            V((depth2, 128), BF), V((maps_pad, depth2), BF),
            V((128, 128), F32), V((8, wide), F32),
            V((128, 128), F32), V((128, up(second_weight.shape[1], 128)), F32),
            V((depth2, 128), F32),
            V((n_s, 8, wide), F32), V((n_s, 8, wide), F32),
            V((n_s, cap_pad, breadth), BF), V((n_s, cap_pad, breadth), BF),
            V((depth2, lanes), BF), V((fields_pad, lanes), F32), V((first_pad, lanes), F32),
            V((3, maps_pad, lanes), F32), V((fields_pad, lanes), F32),
            V((blocks, pair * fields_pad, breadth), BF),
            V((n_s, blocks, pair * fields_pad, breadth), BF),
            V((n_s, cap_pad, breadth), BF), V((n_g, n_s, cap_pad, breadth), BF),
            V((n_g, 8, wide), F32), V((part, breadth), BF), V((n_g, part, breadth), BF),
            dma((5,)), dma((n_s,)), dma((n_s,)), dma((n_s,)), dma((n_s,)),
            dma((blocks, n_s)), dma((blocks, n_s)),
            dma((n_g,)), dma((n_g,)), dma((n_g,)), dma((n_g,)), dma((n_g,)), dma((n_g,)),
            dma((n_s,)), dma((n_s,)),
        ],
        compiler_params=pltpu.CompilerParams(
            collective_id=0, has_side_effects=True, vmem_limit_bytes=VMEM_LIMIT
        ),
        name="step",
    )(
        hot_row, cold_row, cold_owner, is_cold, grad_logit, hot_table, cold_table,
        first_weight, second_weight, third_weight, out_weight,
    )


def solution(mesh):
    rows = P(("group", "shard"), None)
    return jax.shard_map(
        local,
        mesh=mesh,
        in_specs=(
            rows, rows, rows, rows, P(("group", "shard")), P(), P("shard", None),
            P(), P(), P(), P(),
        ),
        out_specs=(P(), P("shard", None), P(("group", "shard"))),
        check_vma=False,
    )
```

```python
import functools

import jax
import jax.numpy as jnp
from jax import lax
from jax.experimental import pallas as pl
from jax.experimental.pallas import tpu as pltpu
from jax.sharding import PartitionSpec as P

BF = jnp.bfloat16
F32 = jnp.float32
MESH = pl.DeviceIdType.MESH
VMEM_LIMIT = 56 * 1024 * 1024


def up(value, unit):
    return (value + unit - 1) // unit * unit


def iota(shape, dim):
    return lax.broadcasted_iota(jnp.int32, shape, dim).astype(F32)


def dot(a, b):
    return jnp.dot(a, b, preferred_element_type=F32)


def dot_t(a, b):
    return lax.dot_general(a, b, (((0,), (0,)), ((), ())), preferred_element_type=F32)


def as_row(col, width):
    rows = col.shape[0]
    hit = iota((rows, width), 0) == iota((rows, width), 1)
    return jnp.sum(jnp.where(hit, col + 1.0, 0.0), axis=0, keepdims=True) - 1.0


def prepare_weight(w_ref, fields, maps_pad, fields_pad, wide, tall, wt_ref, wf_ref):
    high, cols = w_ref.shape
    cols_pad = up(cols, 128)
    total = fields_pad * maps_pad
    wide[...] = jnp.zeros_like(wide)
    wide[0:high, 0:cols] = w_ref[...].astype(F32)
    for b in range(cols_pad // 128):
        tall[b * 128 : (b + 1) * 128, :] = wide[:, b * 128 : (b + 1) * 128].T
    tall[cols_pad:, :] = jnp.zeros((tall.shape[0] - cols_pad, 128), F32)
    for f in range(fields_pad):
        block = slice(f * maps_pad, (f + 1) * maps_pad)
        if f < fields:
            wt_ref[block, :] = tall[pl.ds(f, maps_pad, stride=fields), :].astype(BF)
        else:
            wt_ref[block, :] = jnp.zeros((maps_pad, 128), BF)
    for b in range(total // 128):
        block = wt_ref[b * 128 : (b + 1) * 128, :].astype(F32).T
        wf_ref[:, b * 128 : (b + 1) * 128] = block[0 : wf_ref.shape[0]].astype(BF)


def step_kernel(
    n_g, n_s,
    hot_row, cold_row, cold_owner, is_cold, gl, hot_table, cold_table, w1, w2, w3, ow,
    hot_out, cold_out, logit,
    hot_v, cold_v, w1_v, w2_v, w3_v, emb, wt1, wf1, wt2, wf2, wt3, wf3, owc, meta,
    pack, wide, tall, ask, asked, reply, fetched,
    outer, base, low, states, ge,
    gmine, gall, inc, allin, ids_all, hot_mid, hot_all,
    load_s, ask_s, ask_r, rep_s, rep_r, sp_s, sp_r,
    all_s, all_r, id_s, id_r, hm_s, hm_r, hg_s, hg_r,
):
    me_g, me_s = lax.axis_index("group"), lax.axis_index("shard")
    barrier = pltpu.get_barrier_semaphore()
    for k in range(1, n_s):
        pl.semaphore_signal(
            barrier, inc=1, device_id=(me_g, lax.rem(me_s + k, n_s)), device_id_type=MESH
        )
    for k in range(1, n_g):
        pl.semaphore_signal(
            barrier, inc=1, device_id=(lax.rem(me_g + k, n_g), me_s), device_id_type=MESH
        )
    loads = [
        pltpu.make_async_copy(src, dst, load_s.at[i])
        for i, (src, dst) in enumerate(
            ((hot_table, hot_v), (cold_table, cold_v), (w1, w1_v), (w2, w2_v), (w3, w3_v))
        )
    ]
    for load in loads:
        load.start()
    samples, fields = hot_row.shape
    fields_pad = up(fields, 8)
    looks = samples * fields_pad
    cap_pad = fetched.shape[1]
    slots = n_s * cap_pad
    tight = inc.shape[0] // n_s
    tight_slots = n_s * tight
    hot_rows, shard_rows = hot_out.shape[0], cold_out.shape[0]
    part = hot_rows // n_s
    pair = base.shape[1] // 128
    high = wf1.shape[0]
    wts, wfs = (wt1, wt2, wt3), (wf1, wf2, wf3)

    def shard_copy(k, src, dst, s_sem, r_sem):
        peer = lax.rem(me_s + k, n_s)
        return pltpu.make_async_remote_copy(
            src_ref=src(peer), dst_ref=dst(me_s), send_sem=s_sem.at[k],
            recv_sem=r_sem.at[k], device_id=(me_g, peer), device_id_type=MESH,
        )

    def shard_wait(k, src, dst, s_sem, r_sem):
        peer = lax.rem(me_s + n_s - k, n_s)
        return pltpu.make_async_remote_copy(
            src_ref=src(peer), dst_ref=dst(peer), send_sem=s_sem.at[k],
            recv_sem=r_sem.at[k], device_id=(me_g, peer), device_id_type=MESH,
        )

    def group_copy(k, src, dst, s_sem, r_sem):
        peer = lax.rem(me_g + k, n_g)
        return pltpu.make_async_remote_copy(
            src_ref=src, dst_ref=dst(me_g), send_sem=s_sem.at[k],
            recv_sem=r_sem.at[k], device_id=(peer, me_s), device_id_type=MESH,
        )

    def group_wait(k, src, dst, s_sem, r_sem):
        peer = lax.rem(me_g + n_g - k, n_g)
        return pltpu.make_async_remote_copy(
            src_ref=src, dst_ref=dst(peer), send_sem=s_sem.at[k],
            recv_sem=r_sem.at[k], device_id=(peer, me_s), device_id_type=MESH,
        )

    cold_g = (inc, lambda p: allin.at[p], all_s, all_r)
    id_g = (meta, lambda p: ids_all.at[p], id_s, id_r)
    hot_g = (hot_mid, lambda p: hot_all.at[p], hm_s, hm_r)

    def hot_slice(p):
        return hot_out.at[pl.ds(pl.multiple_of(p * part, part), part)]

    hot_f = (lambda p: hot_slice(me_s), hot_slice, hg_s, hg_r)

    def spread_copy(b, k):
        peer = lax.rem(me_s + k, n_s)
        return pltpu.make_async_remote_copy(
            src_ref=gmine.at[b], dst_ref=gall.at[me_s, b], send_sem=sp_s.at[b, k],
            recv_sem=sp_r.at[b, k], device_id=(me_g, peer), device_id_type=MESH,
        )

    def spread_wait(b, k):
        src = lax.rem(me_s + n_s - k, n_s)
        return pltpu.make_async_remote_copy(
            src_ref=gmine.at[b], dst_ref=gall.at[src, b], send_sem=sp_s.at[b, k],
            recv_sem=sp_r.at[b, k], device_id=(me_g, src), device_id_type=MESH,
        )

    pack[...] = jnp.full(pack.shape, -1.0, F32)
    for a, ref in enumerate((hot_row, cold_row, cold_owner, is_cold)):
        pack[a * samples : (a + 1) * samples, 0:fields] = ref[...].astype(F32)
    turned = pack[...].T

    def column(a):
        return jnp.concatenate(
            [
                turned[0:fields_pad, a * samples + s : a * samples + s + 1]
                for s in range(samples)
            ],
            axis=0,
        )

    hot_c, row_c, owner_c, flag_c = (column(a) for a in range(4))
    cold = flag_c == 1.0
    lanes = iota((looks, 128), 1)
    wanted = jnp.where(jnp.logical_and(owner_c == lanes, cold), 1.0, 0.0)
    lower = jnp.where(iota((looks, looks), 1) < iota((looks, looks), 0), 1.0, 0.0)
    earlier = dot(lower.astype(BF), wanted.astype(BF))
    pos_c = jnp.sum(earlier * wanted, axis=1, keepdims=True)
    target_c = jnp.where(cold, owner_c * cap_pad + pos_c, -1.0)
    at_pos = jnp.where(jnp.logical_and(pos_c == lanes, cold), 1.0, 0.0)
    code = row_c + 1.0
    code_hi = jnp.floor(code * (1.0 / 128.0))
    code_lo = code - code_hi * 128.0
    coded = jnp.concatenate([at_pos * code_hi, at_pos * code_lo], axis=1)
    found = dot_t(wanted.astype(BF), coded.astype(BF))
    ids = found[:, 0:128] * 128.0 + found[:, 128:256] - 1.0
    width = meta.shape[1]
    hot_r = as_row(jnp.where(cold, -1.0, hot_c), width)
    target_r = as_row(target_c, width)
    for o in range(n_s):
        ask[o, 0:1, 0:128] = ids[o : o + 1, :]
        ask[o, 1:2, :] = hot_r
        ask[o, 2:3, :] = target_r

    pl.semaphore_wait(barrier, n_s - 1 + n_g - 1)

    def ask_copy(k):
        peer = lax.rem(me_s + k, n_s)
        return pltpu.make_async_remote_copy(
            src_ref=ask.at[peer], dst_ref=asked.at[me_s], send_sem=ask_s.at[k],
            recv_sem=ask_r.at[k], device_id=(me_g, peer), device_id_type=MESH,
        )

    def ask_wait(k):
        src = lax.rem(me_s + n_s - k, n_s)
        return pltpu.make_async_remote_copy(
            src_ref=ask.at[src], dst_ref=asked.at[src], send_sem=ask_s.at[k],
            recv_sem=ask_r.at[k], device_id=(me_g, src), device_id_type=MESH,
        )

    for k in range(1, n_s):
        ask_copy(k).start()
    asked[me_s] = ask[me_s]

    loads[0].wait()
    at_hot = jnp.logical_and(hot_c == iota((looks, hot_rows), 1), jnp.logical_not(cold))
    hot_part = dot(jnp.where(at_hot, 1.0, 0.0).astype(BF), hot_v[...])
    loads[2].wait()
    prepare_weight(w1_v, fields, wt1.shape[0] // fields_pad, fields_pad, wide, tall, wt1, wf1)

    for k in range(1, n_s):
        ask_wait(k).wait_recv()
    pack[...] = jnp.full(pack.shape, -1.0, F32)
    for d in range(n_s):
        pack[d : d + 1, :] = asked[d, 0:1, 0:128]
    turned2 = pack[...].T
    ids_c = jnp.concatenate([turned2[0:cap_pad, d : d + 1] for d in range(n_s)], axis=0)
    at_row = jnp.where(ids_c == iota((slots, shard_rows), 1), 1.0, 0.0)
    loads[1].wait()
    rows = dot(at_row.astype(BF), cold_v[...]).astype(BF)
    for d in range(n_s):
        reply[d] = rows[d * cap_pad : (d + 1) * cap_pad]

    def rep_copy(k):
        peer = lax.rem(me_s + k, n_s)
        return pltpu.make_async_remote_copy(
            src_ref=reply.at[peer], dst_ref=fetched.at[me_s], send_sem=rep_s.at[k],
            recv_sem=rep_r.at[k], device_id=(me_g, peer), device_id_type=MESH,
        )

    def rep_wait(k):
        src = lax.rem(me_s + n_s - k, n_s)
        return pltpu.make_async_remote_copy(
            src_ref=reply.at[src], dst_ref=fetched.at[src], send_sem=rep_s.at[k],
            recv_sem=rep_r.at[k], device_id=(me_g, src), device_id_type=MESH,
        )

    for k in range(1, n_s):
        rep_copy(k).start()
    fetched[me_s] = reply[me_s]

    tight_c = jnp.concatenate([turned2[0:tight, d : d + 1] for d in range(n_s)], axis=0)
    meta[...] = jnp.broadcast_to(as_row(tight_c, width), meta.shape)
    for k in range(1, n_g):
        group_copy(k, *id_g).start()
    ids_all[me_g] = meta[...]
    loads[3].wait()
    prepare_weight(w2_v, fields, wt2.shape[0] // fields_pad, fields_pad, wide, tall, wt2, wf2)
    loads[4].wait()
    prepare_weight(w3_v, fields, wt3.shape[0] // fields_pad, fields_pad, wide, tall, wt3, wf3)
    pack[...] = jnp.zeros(pack.shape, F32)
    pack[0 : ow.shape[0], 0 : ow.shape[1]] = ow[...]
    owc[...] = pack[...].T

    for k in range(1, n_s):
        rep_wait(k).wait_recv()
    at_slot = jnp.where(target_c == iota((looks, slots), 1), 1.0, 0.0).astype(BF)
    got = jnp.concatenate([fetched[d] for d in range(n_s)], axis=0)
    emb[...] = (dot(at_slot, got) + hot_part).astype(BF)
    for k in range(1, n_s):
        ask_copy(k).wait_send()
        rep_copy(k).wait_send()

    @pl.loop(0, samples // pair)
    def _(b):
        row0 = pl.multiple_of(b * (pair * fields_pad), 8)
        block = emb[pl.ds(row0, pair * fields_pad), :].astype(F32)
        x0 = jnp.concatenate(
            [block[p * fields_pad : (p + 1) * fields_pad] for p in range(pair)], axis=1
        )
        base[...] = x0
        lanes = base.shape[1]
        grow = jnp.concatenate(
            [jnp.full((1, 128), gl[b * pair + p], F32) for p in range(pair)], axis=1
        )
        first_pad = wt1.shape[0] // fields_pad
        low[0:fields_pad, :] = x0
        low[fields_pad:first_pad, :] = jnp.zeros((first_pad - fields_pad, lanes), F32)
        below = low[...]
        inputs = [below]
        total = jnp.zeros((1, lanes), F32)
        for k in range(3):
            maps_pad = wts[k].shape[0] // fields_pad
            below_b = below.astype(BF)
            for f in range(fields_pad):
                start = f * maps_pad
                if f < fields:
                    wide = jnp.broadcast_to(base[f : f + 1, :], (16, lanes)).astype(BF)
                    for t in range(maps_pad // 16):
                        outer[start + t * 16 : start + t * 16 + 16, :] = (
                            below_b[t * 16 : t * 16 + 16] * wide
                        )
                else:
                    outer[start : start + maps_pad, :] = jnp.zeros((maps_pad, lanes), BF)
            depth = fields_pad * maps_pad
            state = dot(wfs[k][...], outer[0:depth, :]).astype(BF).astype(F32)
            total = total + jnp.sum(state * owc[0:high, k : k + 1], axis=0, keepdims=True)
            states[k] = state
            below = state
        for p in range(pair):
            logit[b * pair + p] = jnp.sum(total[:, p * 128 : (p + 1) * 128])

        carried = jnp.zeros((high, lanes), F32)
        chunk = 8
        for k in (2, 1, 0):
            maps_pad = wts[k].shape[0] // fields_pad
            used = fields_pad if k == 0 else up(ow.shape[1], 8)
            grad_state = carried + owc[0:high, k : k + 1] * grow
            grad_low = jnp.concatenate(
                [grad_state.astype(BF), jnp.zeros((128 - high, lanes), BF)], axis=0
            )
            lower = low if k == 0 else states.at[k - 1]
            acc = jnp.zeros((used, lanes), F32)
            for c in range(0, fields, chunk):
                many = min(chunk, fields_pad - c)
                g = dot(wts[k][c * maps_pad : (c + many) * maps_pad, :], grad_low)
                for f in range(c, min(c + many, fields)):
                    gf = g[(f - c) * maps_pad : (f - c) * maps_pad + used]
                    acc = acc + gf * base[f : f + 1, :]
                    part = jnp.sum(gf * lower[0:used, :], axis=0, keepdims=True)
                    if k == 2:
                        ge[f : f + 1, :] = part
                    else:
                        ge[f : f + 1, :] += part
            if k > 0:
                carried = jnp.concatenate(
                    [acc, jnp.zeros((high - used, lanes), F32)], axis=0
                )
            else:
                carried = acc
        out = ge[...] + carried[0:fields_pad]
        keep = lax.broadcasted_iota(jnp.int32, out.shape, 0) < fields
        out = jnp.where(keep, out, 0.0).astype(BF)
        gmine[b] = jnp.concatenate(
            [out[:, p * 128 : (p + 1) * 128] for p in range(pair)], axis=0
        )
        for k in range(1, n_s):
            spread_copy(b, k).start()
        gall[me_s, b] = gmine[b]

    blocks = gmine.shape[0]
    for b in range(blocks):
        for k in range(1, n_s):
            spread_wait(b, k).wait_recv()
    mine = (me_s * part).astype(F32)
    first_slot = (me_s * cap_pad).astype(F32)
    hot_sum = jnp.zeros((part, 128), F32)
    kept = []
    for d in range(n_s):
        terms = jnp.concatenate([gall[d, b] for b in range(blocks)], axis=0)
        hot_r = asked[d, 1:2, 0:looks] - mine
        slot_r = asked[d, 2:3, 0:looks] - first_slot
        at = jnp.concatenate(
            [
                jnp.where(hot_r == iota((part, looks), 0), 1.0, 0.0),
                jnp.where(slot_r == iota((tight, looks), 0), 1.0, 0.0),
            ],
            axis=0,
        )
        both = dot(at.astype(BF), terms)
        hot_sum = hot_sum + both[0:part]
        kept.append(both[part : part + tight])
    hot_mid[...] = hot_sum.astype(BF)
    inc[...] = jnp.concatenate(kept, axis=0).astype(BF)
    for k in range(1, n_g):
        group_copy(k, *hot_g).start()
    for k in range(1, n_g):
        group_copy(k, *cold_g).start()
    hot_all[me_g] = hot_mid[...]
    allin[me_g] = inc[...]

    for k in range(1, n_g):
        group_wait(k, *hot_g).wait_recv()
    total = hot_all[0].astype(F32)
    for d in range(1, n_g):
        total = total + hot_all[d].astype(F32)
    hot_slice(me_s)[...] = total.astype(BF)
    for k in range(1, n_s):
        shard_copy(k, *hot_f).start()

    for k in range(1, n_g):
        group_wait(k, *id_g).wait_recv()
        group_wait(k, *cold_g).wait_recv()
    terms = jnp.concatenate(
        [allin[q] for q in range(n_g)], axis=0
    )
    step = 512 if shard_rows % 512 == 0 else shard_rows

    @pl.loop(0, shard_rows // step)
    def _(t):
        first = pl.multiple_of(t * step, step)
        here = iota((step, tight_slots), 0) + first.astype(F32)
        at = jnp.concatenate(
            [
                jnp.where(ids_all[q][0:1, 0:tight_slots] == here, 1.0, 0.0).astype(BF)
                for q in range(n_g)
            ],
            axis=1,
        )
        cold_out[pl.ds(first, step), :] = dot(at, terms).astype(BF)

    for k in range(1, n_s):
        shard_wait(k, *hot_f).wait_recv()
    for k in range(1, n_s):
        for b in range(blocks):
            spread_copy(b, k).wait_send()
        shard_copy(k, *hot_f).wait_send()
    for k in range(1, n_g):
        group_copy(k, *id_g).wait_send()
        group_copy(k, *cold_g).wait_send()
        group_copy(k, *hot_g).wait_send()


def local(
    hot_row, cold_row, cold_owner, is_cold, grad_logit, hot_table, cold_table,
    first_weight, second_weight, third_weight, out_weight,
):
    n_g, n_s = lax.axis_size("group"), lax.axis_size("shard")
    samples, fields = hot_row.shape
    breadth = hot_table.shape[1]
    maps = out_weight.shape[1]
    cap_pad = up(samples * fields // n_s, 16)
    tight = up(samples * fields // n_s, 8)
    tight = tight if n_s * tight % 16 == 0 else cap_pad
    slots = n_s * cap_pad
    fields_pad = up(fields, 8)
    looks = samples * fields_pad
    first_pad, maps_pad = up(fields_pad, 16), up(maps, 16)
    depth1, depth2 = fields_pad * first_pad, fields_pad * maps_pad
    wide = up(max(slots, looks), 128)
    pair = 2
    lanes = pair * 128
    blocks = samples // pair
    part = hot_table.shape[0] // n_s
    vm = pl.BlockSpec(memory_space=pltpu.VMEM)
    sm = pl.BlockSpec(memory_space=pltpu.SMEM)
    hbm = pl.BlockSpec(memory_space=pl.ANY)
    sd = jax.ShapeDtypeStruct
    dma = pltpu.SemaphoreType.DMA
    V = pltpu.VMEM
    return pl.pallas_call(
        functools.partial(step_kernel, n_g, n_s),
        out_shape=(
            sd(hot_table.shape, BF), sd(cold_table.shape, BF), sd((samples,), F32)
        ),
        in_specs=[vm] * 4 + [sm] + [hbm] * 5 + [vm],
        out_specs=(vm, vm, sm),
        scratch_shapes=[
            V(hot_table.shape, BF), V(cold_table.shape, BF), V(first_weight.shape, BF),
            V(second_weight.shape, BF), V(third_weight.shape, BF),
            V((looks, breadth), BF),
            V((depth1, 128), BF), V((maps_pad, depth1), BF),
            V((depth2, 128), BF), V((maps_pad, depth2), BF),
            V((depth2, 128), BF), V((maps_pad, depth2), BF),
            V((128, 128), F32), V((8, wide), F32),
            V((128, 128), F32), V((128, up(second_weight.shape[1], 128)), F32),
            V((depth2, 128), F32),
            V((n_s, 8, wide), F32), V((n_s, 8, wide), F32),
            V((n_s, cap_pad, breadth), BF), V((n_s, cap_pad, breadth), BF),
            V((depth2, lanes), BF), V((fields_pad, lanes), F32), V((first_pad, lanes), F32),
            V((3, maps_pad, lanes), F32), V((fields_pad, lanes), F32),
            V((blocks, pair * fields_pad, breadth), BF),
            V((n_s, blocks, pair * fields_pad, breadth), BF),
            V((n_s * tight, breadth), BF), V((n_g, n_s * tight, breadth), BF),
            V((n_g, 8, wide), F32), V((part, breadth), BF), V((n_g, part, breadth), BF),
            dma((5,)), dma((n_s,)), dma((n_s,)), dma((n_s,)), dma((n_s,)),
            dma((blocks, n_s)), dma((blocks, n_s)),
            dma((n_g,)), dma((n_g,)), dma((n_g,)), dma((n_g,)), dma((n_g,)), dma((n_g,)),
            dma((n_s,)), dma((n_s,)),
        ],
        compiler_params=pltpu.CompilerParams(
            collective_id=0, has_side_effects=True, vmem_limit_bytes=VMEM_LIMIT
        ),
        name="step",
    )(
        hot_row, cold_row, cold_owner, is_cold, grad_logit, hot_table, cold_table,
        first_weight, second_weight, third_weight, out_weight,
    )


def solution(mesh):
    rows = P(("group", "shard"), None)
    return jax.shard_map(
        local,
        mesh=mesh,
        in_specs=(
            rows, rows, rows, rows, P(("group", "shard")), P(), P("shard", None),
            P(), P(), P(), P(),
        ),
        out_specs=(P(), P("shard", None), P(("group", "shard"))),
        check_vma=False,
    )
```
